32 devices in a mesh: grp: 8 (over z, x), agg: 4 (over y, core).
Axes of the slice: x: 2, y: 2, z: 4, core: 2. Of those that a mesh axis runs over, the one named last changes fastest.
Arguments:
- solution: float32 [128, 32, 128], P('grp', 'agg'), may hold values from -6 to 6
- source_term: float32 [128, 32, 128], P('grp', 'agg'), may hold values from -6 to 6
- face_x: float32 [128, 32, 128], P('grp', 'agg'), may hold values from 0.5 to 2
- face_y: float32 [128, 32, 128], P('grp', 'agg'), may hold values from 0.5 to 2
- face_z: float32 [128, 32, 128], P('grp', 'agg'), may hold values from 0.5 to 2
Outputs:
- correction: float32 [64, 16, 64], P('grp', 'agg')
The draws below stay inside these ranges and needn't reach their ends.
All inputs are finite; a program needn't handle non-finite values.
Results may differ from the reference program's by a relative error of at most 0.0003.
Values sent between devices are 32-bit elements; how exact they have to be, the bound alone decides.
A program may use at most 64 MiB of HBM per device.

```python
import math
import jax
import jax.numpy as jnp

NZ = 128
SWEEPS = 2
MERGES = 2
NX = 128
NY = 32


def level_of(stream_key, shape, cuts, low, high):
    def one(axis_at, shards_of):
        heights = jax.random.uniform(jax.random.fold_in(jax.random.fold_in(stream_key, 6), axis_at), (shards_of,), jnp.float32, low / len(cuts), high / len(cuts))
        return jnp.repeat(jnp.exp(heights), shape[axis_at] // shards_of).reshape((-1,) + (1,) * (len(shape) - axis_at - 1))

    level = one(*cuts[0])
    for cut in cuts[1:]:
        level = level * one(*cut)
    return level


def bell_draw(stream_key, extent, deviation, limit, pieces=(), dtype=jnp.bfloat16):
    result = deviation * jax.random.normal(stream_key, extent, jnp.float32)
    if pieces:
        result = result * level_of(stream_key, extent, pieces, -0.22, 0.18)
    return jnp.clip(result, -limit, limit).astype(dtype)


def setup_inputs(seed: int = 0) -> dict:
    streams_of = jax.random.split(jax.random.key(seed), 6)
    return {
        "solution": bell_draw(streams_of[0], (NX, NY, NZ), 1.0, 6.0, ((0, 8), (1, 4)), jnp.float32),
        "source_term": bell_draw(streams_of[1], (NX, NY, NZ), 1.0, 6.0, ((0, 8), (1, 4)), jnp.float32),
        "face_x": jnp.clip(jnp.exp(math.log(2.0) - 1.3862944 * jax.random.uniform(streams_of[2], (NX, NY, NZ), jnp.float32) ** level_of(streams_of[2], (NX, NY, NZ), ((0, 8), (1, 4)), -0.2, 0.2)), 0.5, 2.0),
        "face_y": jnp.clip(jnp.exp(math.log(2.0) - 1.3862944 * jax.random.uniform(streams_of[3], (NX, NY, NZ), jnp.float32) ** level_of(streams_of[3], (NX, NY, NZ), ((0, 8), (1, 4)), -0.2, 0.2)), 0.5, 2.0),
        "face_z": jnp.clip(jnp.exp(math.log(2.0) - 1.3862944 * jax.random.uniform(streams_of[4], (NX, NY, NZ), jnp.float32) ** level_of(streams_of[4], (NX, NY, NZ), ((0, 8), (1, 4)), -0.2, 0.2)), 0.5, 2.0),
    }


damping = 2.0 / 3.0


def operate(current, coefficients, factor):
    summed = jnp.zeros_like(current)
    diagonal = jnp.zeros_like(current)
    for dimension in range(3):
        face_here = coefficients[dimension]
        face_below = jnp.roll(face_here, 1, dimension)
        value_above = jnp.roll(current, -1, dimension)
        value_below = jnp.roll(current, 1, dimension)
        summed = summed + face_here * (current - value_above) + face_below * (current - value_below)
        diagonal = diagonal + face_here + face_below
    return factor * summed, factor * diagonal


def coarsen(residual, coefficients):
    extent_x, extent_y, extent_z = residual.shape
    shaped = (extent_x // 2, 2, extent_y // 2, 2, extent_z // 2, 2)
    coarse_res = jnp.mean(residual.reshape(shaped), axis=(1, 3, 5))
    along_x = jnp.mean(coefficients[0].reshape(shaped)[:, 1], axis=(2, 4))
    along_y = jnp.mean(coefficients[1].reshape(shaped)[:, :, :, 1], axis=(1, 4))
    along_z = jnp.mean(coefficients[2].reshape(shaped)[..., 1], axis=(1, 3))
    return coarse_res, (along_x, along_y, along_z)


def smooth(current, residual, coefficients, factor):
    for repeat in range(SWEEPS):
        applied, diagonal = operate(current, coefficients, factor)
        current = current + damping * (residual - applied) / diagonal
    return current


def eigenvalues(count_all):
    wavenumbers = jnp.arange(count_all).astype(jnp.float32)
    return 2.0 - 2.0 * jnp.cos(2.0 * jnp.pi * wavenumbers / count_all)


def spectral_solve(source, factor):
    count_x, count_y, count_z = source.shape
    symbol = factor * (eigenvalues(count_x)[:, None, None] + eigenvalues(count_y)[None, :, None] + eigenvalues(count_z)[None, None, :])
    anchor = (jnp.arange(count_x)[:, None, None] == 0) & (jnp.arange(count_y)[None, :, None] == 0) & (jnp.arange(count_z)[None, None, :] == 0)
    safe_symbol = jnp.where(anchor, 1.0, symbol)
    spectrum = jnp.fft.fftn(source)
    solved = jnp.where(anchor, 0.0, spectrum / safe_symbol)
    return jnp.real(jnp.fft.ifftn(solved)).astype(jnp.float32)


def reference(solution, source_term, face_x, face_y, face_z):
    coefficients = (face_x, face_y, face_z)
    applied = operate(solution, coefficients, 1.0)[0]
    residual = source_term - applied
    hierarchy = []
    for level_index in range(MERGES):
        residual, coefficients = coarsen(residual, coefficients)
        hierarchy.append((residual, coefficients))
    bottom_res, bottom_coef = hierarchy[-1]
    middle_res, middle_coef = hierarchy[-2]
    bottom_factor = 0.25 ** MERGES
    current = spectral_solve(bottom_res, bottom_factor)
    current = smooth(current, bottom_res, bottom_coef, bottom_factor)
    current = jnp.repeat(jnp.repeat(jnp.repeat(current, 2, 0), 2, 1), 2, 2)
    return smooth(current, middle_res, middle_coef, 0.25 ** (MERGES - 1))
```

```python
import functools

import jax
import jax.numpy as jnp
import ml_dtypes
import numpy as np
from jax import lax
from jax.experimental import pallas as pl
from jax.experimental.pallas import tpu as pltpu
from jax.sharding import PartitionSpec as P

LANES = 128
SWEEPS = 2
MESH = pl.DeviceIdType.MESH


class Sizes:
    def __init__(self, groups, members, block):
        self.G, self.A = groups, members
        self.X, self.Y, self.Z = block
        self.merges = members.bit_length() - 1
        self.f = 2 ** (self.merges - 1)
        self.b = 2**self.merges
        self.xm, self.ym, self.zm = self.X // self.f, self.Y // self.f, self.Z // self.f
        self.xb, self.zb = self.X // self.b, self.Z // self.b
        self.yb = max(1, self.Y // self.b)
        self.YM, self.YB = self.A * self.ym, self.A * self.Y // self.b
        self.q = self.A * self.yb // self.YB
        self.h = -(-(SWEEPS + 1) // self.xb)
        self.S = 2 * self.h + 1
        self.NXB = self.G * self.xb
        self.XBP = -(-self.S * self.xb // 8) * 8
        self.XMP = -(-(self.xm + 2 * SWEEPS) // 8) * 8
        self.RM = -(-self.ym * self.xm // 8) * 8
        self.RB = -(-self.yb * self.xb // 8) * 8
        self.per = LANES // self.zb
        self.NL = self.A * self.yb * self.zb // LANES


def bf16_parts(table):
    first = table.astype(ml_dtypes.bfloat16)
    second = (table - first.astype(np.float64)).astype(ml_dtypes.bfloat16)
    return np.stack([first, second])


def real_basis(count):
    at = np.arange(count)[:, None]
    mode = np.arange(count)
    wave = (mode + 1) // 2
    angle = 2 * np.pi * ((at * wave[None, :]) % count) / count
    basis = np.where(mode[None, :] % 2 == 1, np.cos(angle), np.sin(angle)) * np.sqrt(2.0 / count)
    basis[:, 0] = np.sqrt(1.0 / count)
    if count % 2 == 0:
        basis[:, count - 1] = np.sqrt(1.0 / count) * (1 - 2 * (np.arange(count) % 2))
    return basis, wave


def tables(s):
    left = np.zeros((4, s.RM + s.RB, s.X * s.Y))
    for x in range(s.X):
        for y in range(s.Y):
            for base, f, xn, in ((0, s.f, s.xm), (s.RM, s.b, s.xb)):
                row, col = base + (y // f) * xn + x // f, x * s.Y + y
                last_x, last_y = x % f == f - 1, y % f == f - 1 or (f > s.Y and y == s.Y - 1)
                left[0, row, col] = 1 / f**2
                left[1, row, col] = last_x / f
                left[2, row, col] = last_y / f
                left[3, row, col] = 1 / f**2
    right = np.zeros((2, s.Z, 2 * LANES))
    for lane in range(LANES):
        for base, f, zn in ((0, s.f, s.zm), (LANES, s.b, s.zb)):
            z = lane % zn
            right[0, z * f : (z + 1) * f, base + lane] = 1 / f
            right[1, (z + 1) * f - 1, base + lane] = 1
    qx, wx = real_basis(s.NXB)
    qy, wy = real_basis(s.YB)
    qz, wz = real_basis(s.zb)
    rows = np.arange(s.A * s.yb) // s.q
    to_modes = np.einsum("yk,zl->yzkl", qy[rows], qz).reshape(s.NL * LANES, s.YB * s.zb)
    copies = np.arange(LANES) % s.zb
    from_modes = np.einsum("yk,zl->klyz", qy, qz[copies]).reshape(s.YB * s.zb, s.YB * LANES)
    spread = np.einsum("ay,zl->azyl", rows[:, None] == np.arange(s.YB), np.arange(s.zb)[:, None] == copies[None, :])
    spread = spread.reshape(s.NL * LANES, s.YB * LANES).astype(np.float64)

    def eigen(wave, count):
        return 2.0 - 2.0 * np.cos(2.0 * np.pi * wave / count)

    symbol = (
        eigen(wx, s.NXB)[:, None, None] + eigen(wy, s.YB)[None, :, None] + eigen(wz, s.zb)[None, None, :]
    ).reshape(s.NXB, -1) * 0.25**s.merges
    symbol[0, 0] = 1.0
    inverse = 1.0 / symbol
    inverse[0, 0] = 0.0
    near = (np.arange(s.G)[:, None] * s.xb - s.h * s.xb + np.arange(s.XBP)[None, :]) % s.NXB
    qx_near = qx[near]
    pick = (near[:, :, None] == np.arange(s.NXB)).astype(np.float32)
    from_x = np.concatenate([qx_near, pick], 2).astype(np.float32)
    grow_x = np.zeros((s.XMP, s.XBP))
    for row in range(s.XMP):
        grow_x[row, min(s.h * s.xb + (row - SWEEPS) // 2, s.XBP - 1)] = 1
    grow_x = np.kron(np.eye(s.YB), grow_x)
    grow_z = np.zeros((LANES, LANES))
    for lane in range(LANES):
        grow_z[(lane % s.zm) // 2, lane] = 1
    bf = lambda t: t.astype(ml_dtypes.bfloat16)
    return (
        bf(left), bf(right), bf16_parts(to_modes), bf16_parts(from_modes), bf(spread),
        qx.T.astype(np.float32), inverse.astype(np.float32), from_x, bf(grow_x), bf(grow_z),
    )


def cut(value, count):
    parts = []
    for _ in range(count):
        part = value.astype(jnp.bfloat16).astype(jnp.float32)
        parts.append(part)
        value = value - part
    return parts


def dot(one, two):
    return jnp.dot(one, two, preferred_element_type=jnp.float32)


def right_exact(value, table, count=3):
    rows = value.shape[0]
    product = dot(jnp.concatenate(cut(value, count), 0).astype(jnp.bfloat16), table)
    return sum(product[i * rows : (i + 1) * rows] for i in reversed(range(count)))


def left_exact(table, value, count=3):
    columns = value.shape[1]
    product = dot(table, jnp.concatenate(cut(value, count), 1).astype(jnp.bfloat16))
    return sum(product[:, i * columns : (i + 1) * columns] for i in reversed(range(count)))


def right_parts(value, high, low):
    rows = value.shape[0]
    stacked = jnp.concatenate(cut(value, 2), 0).astype(jnp.bfloat16)
    by_high = dot(stacked, high)
    by_low = dot(stacked, low)
    return by_low[:rows] + by_high[rows:] + by_low[rows:] + by_high[:rows]


def full_dot(one, two):
    return jnp.dot(one, two, precision=lax.Precision.HIGHEST, preferred_element_type=jnp.float32)


def turned(value, step, axis):
    if axis == 0:
        return jnp.concatenate([value[step:], value[:step]], 0)
    return pltpu.roll(value, (-step) % value.shape[axis], axis)


def sweeps(current, residual, faces, factor):
    along = (1, 0, 2)
    below = [turned(face, -1, d) for face, d in zip(faces, along)]
    diagonal = sum(face + under for face, under in zip(faces, below))
    scale = (2.0 / 3.0) / (factor * diagonal)
    for _ in range(SWEEPS):
        applied = diagonal * current
        for face, under, d in zip(faces, below, along):
            applied = applied - face * turned(current, 1, d) - under * turned(current, -1, d)
        current = current + scale * (residual - factor * applied)
    return current


def each(count, body):
    if count <= 64:
        for i in range(count):
            body(i)
    else:
        lax.fori_loop(0, count, lambda i, c: (body(i), c)[1], 0)


def kernel(
    s, sol, src, fx, fy, fz,
    left, right, to_modes, from_modes, spread, qx_t, inverse, from_x, grow_x, grow_z,
    out,
    x_low, x_high, y_low, y_high, y_low_src, y_high_src,
    coef_own, coef_side, coef_side_src, coef_bot,
    res_own, res_side, res_side_src, gathered,
    bottom_all, mid_faces, mid_res, bot_faces, final,
    send, recv,
):
    g, a = lax.axis_index("grp"), lax.axis_index("agg")
    me = g * s.A + a
    others = s.G * s.A - 1

    def shifted(i):
        at = lax.rem(me + 1 + i, s.G * s.A)
        return {"grp": at // s.A, "agg": lax.rem(at, s.A)}

    barrier = pltpu.get_barrier_semaphore()
    each(others, lambda i: pl.semaphore_signal(barrier, inc=1, device_id=shifted(i), device_id_type=MESH))

    y_low_src[0] = sol[:, s.Y - 1, :]
    y_low_src[1] = fy[:, s.Y - 1, :]
    y_high_src[...] = sol[:, 0, :]

    def put(src_ref, dst_ref, kind, to):
        copy = pltpu.make_async_remote_copy(
            src_ref=src_ref, dst_ref=dst_ref, send_sem=send.at[kind], recv_sem=recv.at[kind],
            device_id=to, device_id_type=MESH,
        )
        copy.start()

    up, down = lax.rem(g + 1, s.G), lax.rem(g + s.G - 1, s.G)
    right_of, left_of = lax.rem(a + 1, s.A), lax.rem(a + s.A - 1, s.A)

    pl.semaphore_wait(barrier, others)
    put(sol.at[s.X - 1], x_low.at[0], 0, {"grp": up, "agg": a})
    put(fx.at[s.X - 1], x_low.at[1], 1, {"grp": up, "agg": a})
    put(sol.at[0], x_high, 2, {"grp": down, "agg": a})
    put(y_low_src, y_low, 3, {"grp": g, "agg": right_of})
    put(y_high_src, y_high, 4, {"grp": g, "agg": left_of})

    flat = lambda ref: ref[...].reshape(s.X * s.Y, s.Z)
    half = s.RM + s.RB
    rows = [left_exact(left[d + 1], flat(ref)) for d, ref in enumerate((fx, fy, fz))]
    both = right_exact(jnp.concatenate(rows[:2], 0), right[0])
    coarse = [both[:half], both[half:], right_exact(rows[2], right[1])]
    for d in range(3):
        mid, bottom = coarse[d][: s.RM, :LANES], coarse[d][s.RM :, LANES:]
        if d == 1 and s.q > 1:
            bottom = jnp.where(lax.rem(a, s.q) == s.q - 1, bottom, 0.0)
        for y in range(s.ym):
            plane = mid[y * s.xm : (y + 1) * s.xm]
            coef_own[a * s.ym + y, d] = plane
            coef_side_src[0, y, d] = plane[s.xm - SWEEPS :]
            coef_side_src[1, y, d] = plane[:SWEEPS]
        for y in range(s.yb):
            coef_bot[(s.h * s.A + a) * s.yb + y, d] = bottom[y * s.xb : (y + 1) * s.xb]

    own_rows = pl.ds(a * s.ym, s.ym)
    bot_rows = lambda k: pl.ds((k * s.A + a) * s.yb, s.yb)

    def to_members(body):
        each(s.A - 1, lambda i: body({"grp": g, "agg": lax.rem(a + 1 + i, s.A)}))

    def to_sides(body):
        for side, to in ((0, up), (1, down)):
            each(s.A, lambda i: body(side, {"grp": to, "agg": lax.rem(a + i, s.A)}))

    to_sides(lambda side, to: put(coef_side_src.at[side], coef_side.at[side, own_rows], 5, to))
    to_members(lambda to: put(coef_own.at[own_rows], coef_own.at[own_rows], 6, to))
    bot_src = coef_bot.at[bot_rows(s.h)]
    for d in range(-s.h, s.h + 1):
        to_g = lax.rem(g + d + s.G, s.G)
        send_bot = lambda to: put(bot_src, coef_bot.at[bot_rows(s.h - d)], 7, to)
        if d == 0:
            to_members(send_bot)
        else:
            each(s.A, lambda i: send_bot({"grp": to_g, "agg": lax.rem(a + i, s.A)}))

    def got(ref, kind, sems=recv):
        pltpu.make_async_copy(ref, ref, sems.at[kind]).wait()

    here = sol[...]
    f_x, f_y, f_z = fx[...], fy[...], fz[...]
    z_part = f_z * (here - pltpu.roll(here, s.Z - 1, 2))
    z_part = z_part - pltpu.roll(z_part, 1, 2)
    got(x_low.at[0], 0)
    got(x_low.at[1], 1)
    got(x_high, 2)
    flux = f_x * (here - jnp.concatenate([here[1:], x_high[...][None]], 0))
    edge = x_low[1] * (x_low[0] - here[0])
    x_part = flux - jnp.concatenate([edge[None], flux[:-1]], 0)
    got(y_low, 3)
    got(y_high, 4)
    row = lax.broadcasted_iota(jnp.int32, here.shape, 1)
    above = jnp.where(row == s.Y - 1, y_high[...][:, None, :], pltpu.roll(here, s.Y - 1, 1))
    flux = f_y * (here - above)
    edge = (y_low[1] * (y_low[0] - here[:, 0, :]))[:, None, :]
    y_part = flux - jnp.where(row == 0, edge, pltpu.roll(flux, 1, 1))
    residual = src[...] - (x_part + y_part + z_part)

    coarse_res = right_exact(left_exact(left[0], residual.reshape(s.X * s.Y, s.Z)), right[0])
    mid, bottom = coarse_res[: s.RM, :LANES], coarse_res[s.RM :, LANES:]
    group = lax.broadcasted_iota(jnp.int32, (s.xb, LANES), 1) // s.zb
    slot = jnp.zeros((s.xb, LANES), jnp.float32)
    for y in range(s.yb):
        slot = slot + jnp.where(
            group == lax.rem(a * s.yb + y, s.per), bottom[y * s.xb : (y + 1) * s.xb], 0.0
        )
    gathered[me] = slot
    each(others, lambda i: put(gathered.at[me], gathered.at[me], 10, shifted(i)))
    for y in range(s.ym):
        plane = mid[y * s.xm : (y + 1) * s.xm]
        res_own[a * s.ym + y] = plane
        res_side_src[0, y] = plane[s.xm - SWEEPS :]
        res_side_src[1, y] = plane[:SWEEPS]
    to_sides(lambda side, to: put(res_side_src.at[side], res_side.at[side, own_rows], 8, to))
    to_members(lambda to: put(res_own.at[own_rows], res_own.at[own_rows], 9, to))

    got(coef_side, 5)
    part = coef_own.at[pl.ds(0, (s.A - 1) * s.ym)]
    got(part, 6)
    got(coef_bot.at[pl.ds(0, (s.S * s.A - 1) * s.yb)], 7)
    mid_faces[...] = jnp.ones(mid_faces.shape, jnp.float32)
    bot_faces[...] = jnp.ones(bot_faces.shape, jnp.float32)
    for d in range(3):
        mid_faces[d, :, 0:SWEEPS, :] = coef_side[0, :, d]
        mid_faces[d, :, SWEEPS : SWEEPS + s.xm, :] = coef_own[:, d]
        mid_faces[d, :, SWEEPS + s.xm : 2 * SWEEPS + s.xm, :] = coef_side[1, :, d]
        for k in range(s.S):
            for y in range(s.YB):
                total = coef_bot[k * s.A * s.yb + y * s.q, d]
                for i in range(1, s.q):
                    total = total + coef_bot[k * s.A * s.yb + y * s.q + i, d]
                bot_faces[d, y, k * s.xb : (k + 1) * s.xb, :] = total

    got(gathered.at[pl.ds(0, others)], 10)
    chunk = s.A // s.NL
    for i in range(s.G):
        for k in range(s.NL):
            total = gathered[i * s.A + k * chunk]
            for j in range(1, chunk):
                total = total + gathered[i * s.A + k * chunk + j]
            bottom_all[i * s.xb : (i + 1) * s.xb, k * LANES : (k + 1) * LANES] = total
    everything = bottom_all[...]
    modes = right_parts(everything, to_modes[0], to_modes[1])
    modes = full_dot(qx_t[...], modes) * inverse[...]
    near = from_x[g]
    field = right_parts(full_dot(near[:, : s.NXB], modes), from_modes[0], from_modes[1])
    source = right_exact(full_dot(near[:, s.NXB :], everything), spread[...])
    planes = lambda wide: jnp.stack([wide[:, y * LANES : (y + 1) * LANES] for y in range(s.YB)])
    field = sweeps(planes(field), planes(source), [bot_faces[d] for d in range(3)], 0.25**s.merges)

    field = right_exact(field.reshape(s.YB * s.XBP, LANES), grow_z[...])
    field = left_exact(grow_x[...], field).reshape(s.YB, s.XMP, LANES)
    field = jnp.stack([field[y // 2] for y in range(s.YM)])
    got(res_side, 8)
    got(res_own.at[pl.ds(0, (s.A - 1) * s.ym)], 9)
    mid_res[...] = jnp.zeros(mid_res.shape, jnp.float32)
    mid_res[:, 0:SWEEPS, :] = res_side[0]
    mid_res[:, SWEEPS : SWEEPS + s.xm, :] = res_own[...]
    mid_res[:, SWEEPS + s.xm : 2 * SWEEPS + s.xm, :] = res_side[1]
    final[...] = sweeps(field, mid_res[...], [mid_faces[d] for d in range(3)], 0.25 ** (s.merges - 1))
    out[...] = final[own_rows, SWEEPS : SWEEPS + s.xm, : s.zm]

    sent = (
        x_high, x_high, x_high, y_low, y_high, coef_side, part, coef_bot.at[pl.ds(0, (s.S * s.A - 1) * s.yb)],
        res_side, res_own.at[pl.ds(0, (s.A - 1) * s.ym)], gathered.at[pl.ds(0, others)],
    )
    for kind, ref in enumerate(sent):
        got(ref, kind, send)


def local(s, constants, sol, src, fx, fy, fz):
    f32 = lambda *shape: pltpu.VMEM(shape, jnp.float32)
    total = s.G * s.A
    result = pl.pallas_call(
        functools.partial(kernel, s),
        out_shape=jax.ShapeDtypeStruct((s.ym, s.xm, s.zm), jnp.float32),
        in_specs=[pl.BlockSpec(memory_space=pltpu.VMEM)] * (5 + len(constants)),
        out_specs=pl.BlockSpec(memory_space=pltpu.VMEM),
        scratch_shapes=[
            f32(2, s.Y, s.Z), f32(s.Y, s.Z), f32(2, s.X, s.Z), f32(s.X, s.Z), f32(2, s.X, s.Z), f32(s.X, s.Z),
            f32(s.YM, 3, s.xm, LANES), f32(2, s.YM, 3, SWEEPS, LANES), f32(2, s.ym, 3, SWEEPS, LANES),
            f32(s.S * s.A * s.yb, 3, s.xb, LANES),
            f32(s.YM, s.xm, LANES), f32(2, s.YM, SWEEPS, LANES), f32(2, s.ym, SWEEPS, LANES),
            f32(total, s.xb, LANES),
            f32(s.NXB, s.NL * LANES), f32(3, s.YM, s.XMP, LANES), f32(s.YM, s.XMP, LANES),
            f32(3, s.YB, s.XBP, LANES), f32(s.YM, s.XMP, LANES),
            pltpu.SemaphoreType.DMA((11,)),
            pltpu.SemaphoreType.DMA((11,)),
        ],
        compiler_params=pltpu.CompilerParams(
            collective_id=0, has_side_effects=True, vmem_limit_bytes=40 * 1024 * 1024
        ),
    )(sol, src, fx, fy, fz, *constants)
    return jnp.transpose(result, (1, 0, 2))


def solution(mesh):
    groups, members = mesh.shape["grp"], mesh.shape["agg"]

    def whole(*arrays):
        nx, ny, nz = arrays[0].shape
        s = Sizes(groups, members, (nx // groups, ny // members, nz))
        constants = [jnp.asarray(t) for t in tables(s)]
        return jax.shard_map(
            functools.partial(local, s, constants),
            mesh=mesh,
            in_specs=(P("grp", "agg", None),) * 5,
            out_specs=P("grp", "agg", None),
            check_vma=False,
        )(*arrays)

    return whole
```

```python
import functools

import jax
import jax.numpy as jnp
import ml_dtypes
import numpy as np
from jax import lax
from jax.experimental import pallas as pl
from jax.experimental.pallas import tpu as pltpu
from jax.sharding import PartitionSpec as P

LANES = 128
SWEEPS = 2
MESH = pl.DeviceIdType.MESH


class Sizes:
    def __init__(self, groups, members, block):
        self.G, self.A = groups, members
        self.X, self.Y, self.Z = block
        self.merges = members.bit_length() - 1
        self.f = 2 ** (self.merges - 1)
        self.b = 2**self.merges
        self.xm, self.ym, self.zm = self.X // self.f, self.Y // self.f, self.Z // self.f
        self.xb, self.zb = self.X // self.b, self.Z // self.b
        self.yb = max(1, self.Y // self.b)
        self.YM, self.YB = self.A * self.ym, self.A * self.Y // self.b
        self.q = self.A * self.yb // self.YB
        self.h = -(-(SWEEPS + 1) // self.xb)
        self.S = 2 * self.h + 1
        self.NXB = self.G * self.xb
        self.XBP = -(-self.S * self.xb // 8) * 8
        self.XMP = -(-(self.xm + 2 * SWEEPS) // 8) * 8
        self.RM = -(-self.ym * self.xm // 8) * 8
        self.RB = -(-self.yb * self.xb // 8) * 8
        self.per = LANES // self.zb
        self.NL = self.A * self.yb * self.zb // LANES


def bf16_parts(table):
    first = table.astype(ml_dtypes.bfloat16)
    second = (table - first.astype(np.float64)).astype(ml_dtypes.bfloat16)
    return np.stack([first, second])


def real_basis(count):
    at = np.arange(count)[:, None]
    mode = np.arange(count)
    wave = (mode + 1) // 2
    angle = 2 * np.pi * ((at * wave[None, :]) % count) / count
    basis = np.where(mode[None, :] % 2 == 1, np.cos(angle), np.sin(angle)) * np.sqrt(2.0 / count)
    basis[:, 0] = np.sqrt(1.0 / count)
    if count % 2 == 0:
        basis[:, count - 1] = np.sqrt(1.0 / count) * (1 - 2 * (np.arange(count) % 2))
    return basis, wave


def tables(s):
    left = np.zeros((4, s.RM + s.RB, s.X * s.Y))
    for x in range(s.X):
        for y in range(s.Y):
            for base, f, xn, in ((0, s.f, s.xm), (s.RM, s.b, s.xb)):
                row, col = base + (y // f) * xn + x // f, x * s.Y + y
                last_x, last_y = x % f == f - 1, y % f == f - 1 or (f > s.Y and y == s.Y - 1)
                left[0, row, col] = 1 / f**2
                left[1, row, col] = last_x / f
                left[2, row, col] = last_y / f
                left[3, row, col] = 1 / f**2
    right = np.zeros((2, s.Z, 2 * LANES))
    for lane in range(LANES):
        for base, f, zn in ((0, s.f, s.zm), (LANES, s.b, s.zb)):
            z = lane % zn
            right[0, z * f : (z + 1) * f, base + lane] = 1 / f
            right[1, (z + 1) * f - 1, base + lane] = 1
    qx, wx = real_basis(s.NXB)
    qy, wy = real_basis(s.YB)
    qz, wz = real_basis(s.zb)
    rows = np.arange(s.A * s.yb) // s.q
    to_modes = np.einsum("yk,zl->yzkl", qy[rows], qz).reshape(s.NL * LANES, s.YB * s.zb)
    copies = np.arange(LANES) % s.zb
    from_modes = np.einsum("yk,zl->klyz", qy, qz[copies]).reshape(s.YB * s.zb, s.YB * LANES)
    spread = np.einsum("ay,zl->azyl", rows[:, None] == np.arange(s.YB), np.arange(s.zb)[:, None] == copies[None, :])
    spread = spread.reshape(s.NL * LANES, s.YB * LANES).astype(np.float64)

    def eigen(wave, count):
        return 2.0 - 2.0 * np.cos(2.0 * np.pi * wave / count)

    symbol = (
        eigen(wx, s.NXB)[:, None, None] + eigen(wy, s.YB)[None, :, None] + eigen(wz, s.zb)[None, None, :]
    ).reshape(s.NXB, -1) * 0.25**s.merges
    symbol[0, 0] = 1.0
    inverse = 1.0 / symbol
    inverse[0, 0] = 0.0
    near = (np.arange(s.G)[:, None] * s.xb - s.h * s.xb + np.arange(s.XBP)[None, :]) % s.NXB
    qx_near = qx[near]
    pick = (near[:, :, None] == np.arange(s.NXB)).astype(np.float32)
    from_x = np.concatenate([qx_near, pick], 2).astype(np.float32)
    grow_x = np.zeros((s.XMP, s.XBP))
    for row in range(s.XMP):
        grow_x[row, min(s.h * s.xb + (row - SWEEPS) // 2, s.XBP - 1)] = 1
    grow_x = np.kron(np.eye(s.YB), grow_x)
    grow_z = np.zeros((LANES, LANES))
    for lane in range(LANES):
        grow_z[(lane % s.zm) // 2, lane] = 1
    bf = lambda t: t.astype(ml_dtypes.bfloat16)
    return (
        bf(left), bf(right), bf16_parts(to_modes), bf16_parts(from_modes), bf(spread),
        qx.T.astype(np.float32), inverse.astype(np.float32), from_x, bf(grow_x), bf(grow_z),
    )


def cut(value, count):
    parts = []
    for _ in range(count):
        part = value.astype(jnp.bfloat16).astype(jnp.float32)
        parts.append(part)
        value = value - part
    return parts


def dot(one, two):
    return jnp.dot(one, two, preferred_element_type=jnp.float32)


def right_exact(value, table, count=3):
    rows = value.shape[0]
    product = dot(jnp.concatenate(cut(value, count), 0).astype(jnp.bfloat16), table)
    return sum(product[i * rows : (i + 1) * rows] for i in reversed(range(count)))


def left_exact(table, value, count=3):
    columns = value.shape[1]
    product = dot(table, jnp.concatenate(cut(value, count), 1).astype(jnp.bfloat16))
    return sum(product[:, i * columns : (i + 1) * columns] for i in reversed(range(count)))


def right_parts(value, high, low):
    rows = value.shape[0]
    stacked = jnp.concatenate(cut(value, 2), 0).astype(jnp.bfloat16)
    by_high = dot(stacked, high)
    by_low = dot(stacked, low)
    return by_low[:rows] + by_high[rows:] + by_low[rows:] + by_high[:rows]


def full_dot(one, two):
    return jnp.dot(one, two, precision=lax.Precision.HIGHEST, preferred_element_type=jnp.float32)


def turned(value, step, axis):
    if axis == 0:
        return jnp.concatenate([value[step:], value[:step]], 0)
    return pltpu.roll(value, (-step) % value.shape[axis], axis)


def sweeps(current, residual, faces, factor):
    along = (1, 0, 2)
    below = [turned(face, -1, d) for face, d in zip(faces, along)]
    diagonal = sum(face + under for face, under in zip(faces, below))
    scale = (2.0 / 3.0) / (factor * diagonal)
    for _ in range(SWEEPS):
        applied = diagonal * current
        for face, under, d in zip(faces, below, along):
            applied = applied - face * turned(current, 1, d) - under * turned(current, -1, d)
        current = current + scale * (residual - factor * applied)
    return current


def each(count, body):
    if count <= 64:
        for i in range(count):
            body(i)
    else:
        lax.fori_loop(0, count, lambda i, c: (body(i), c)[1], 0)


def kernel(
    s, operand_count, *refs
):
    operands, out, held = refs[:operand_count], refs[operand_count], refs[operand_count + 1 : 2 * operand_count + 1]
    body(s, operands, out, held, *refs[2 * operand_count + 1 :])


def body(
    s, operands, out, held,
    x_low, x_high, y_low, y_high, y_low_src, y_high_src,
    coef_own, coef_side, coef_side_src, coef_bot,
    res_own, res_side, res_side_src, gathered,
    bottom_all, mid_faces, mid_res, bot_faces, final,
    send, recv, loaded,
):
    sol, src, fx, fy, fz, left, right, to_modes, from_modes, spread, qx_t, inverse, from_x, grow_x, grow_z = held
    g, a = lax.axis_index("grp"), lax.axis_index("agg")
    me = g * s.A + a
    others = s.G * s.A - 1

    def shifted(i):
        at = lax.rem(me + 1 + i, s.G * s.A)
        return {"grp": at // s.A, "agg": lax.rem(at, s.A)}

    barrier = pltpu.get_barrier_semaphore()
    each(others, lambda i: pl.semaphore_signal(barrier, inc=1, device_id=shifted(i), device_id_type=MESH))

    order = (0, 3, 2, 4, 5, 6, 1, 7, 10, 11, 12, 8, 9, 13, 14)
    loads = [pltpu.make_async_copy(operands[i], held[i], loaded.at[i]) for i in range(len(held))]
    for i in order:
        loads[i].start()

    def ready(*which):
        for i in which:
            loads[i].wait()

    ready(0, 3)
    y_low_src[0] = sol[:, s.Y - 1, :]
    y_low_src[1] = fy[:, s.Y - 1, :]
    y_high_src[...] = sol[:, 0, :]

    def put(src_ref, dst_ref, kind, to):
        copy = pltpu.make_async_remote_copy(
            src_ref=src_ref, dst_ref=dst_ref, send_sem=send.at[kind], recv_sem=recv.at[kind],
            device_id=to, device_id_type=MESH,
        )
        copy.start()

    up, down = lax.rem(g + 1, s.G), lax.rem(g + s.G - 1, s.G)
    right_of, left_of = lax.rem(a + 1, s.A), lax.rem(a + s.A - 1, s.A)

    ready(2)
    pl.semaphore_wait(barrier, others)
    put(sol.at[s.X - 1], x_low.at[0], 0, {"grp": up, "agg": a})
    put(fx.at[s.X - 1], x_low.at[1], 1, {"grp": up, "agg": a})
    put(sol.at[0], x_high, 2, {"grp": down, "agg": a})
    put(y_low_src, y_low, 3, {"grp": g, "agg": right_of})
    put(y_high_src, y_high, 4, {"grp": g, "agg": left_of})

    ready(4, 5, 6)
    flat = lambda ref: ref[...].reshape(s.X * s.Y, s.Z)
    half = s.RM + s.RB
    rows = [left_exact(left[d + 1], flat(ref)) for d, ref in enumerate((fx, fy, fz))]
    both = right_exact(jnp.concatenate(rows[:2], 0), right[0])
    coarse = [both[:half], both[half:], right_exact(rows[2], right[1])]
    for d in range(3):
        mid, bottom = coarse[d][: s.RM, :LANES], coarse[d][s.RM :, LANES:]
        if d == 1 and s.q > 1:
            bottom = jnp.where(lax.rem(a, s.q) == s.q - 1, bottom, 0.0)
        for y in range(s.ym):
            plane = mid[y * s.xm : (y + 1) * s.xm]
            coef_own[a * s.ym + y, d] = plane
            coef_side_src[0, y, d] = plane[s.xm - SWEEPS :]
            coef_side_src[1, y, d] = plane[:SWEEPS]
        for y in range(s.yb):
            coef_bot[(s.h * s.A + a) * s.yb + y, d] = bottom[y * s.xb : (y + 1) * s.xb]

    own_rows = pl.ds(a * s.ym, s.ym)
    bot_rows = lambda k: pl.ds((k * s.A + a) * s.yb, s.yb)

    def to_members(body):
        each(s.A - 1, lambda i: body({"grp": g, "agg": lax.rem(a + 1 + i, s.A)}))

    def to_sides(body):
        for side, to in ((0, up), (1, down)):
            each(s.A, lambda i: body(side, {"grp": to, "agg": lax.rem(a + i, s.A)}))

    to_sides(lambda side, to: put(coef_side_src.at[side], coef_side.at[side, own_rows], 5, to))
    to_members(lambda to: put(coef_own.at[own_rows], coef_own.at[own_rows], 6, to))
    bot_src = coef_bot.at[bot_rows(s.h)]
    for d in range(-s.h, s.h + 1):
        to_g = lax.rem(g + d + s.G, s.G)
        send_bot = lambda to: put(bot_src, coef_bot.at[bot_rows(s.h - d)], 7, to)
        if d == 0:
            to_members(send_bot)
        else:
            each(s.A, lambda i: send_bot({"grp": to_g, "agg": lax.rem(a + i, s.A)}))

    def got(ref, kind, sems=recv):
        pltpu.make_async_copy(ref, ref, sems.at[kind]).wait()

    here = sol[...]
    f_x, f_y, f_z = fx[...], fy[...], fz[...]
    z_part = f_z * (here - pltpu.roll(here, s.Z - 1, 2))
    z_part = z_part - pltpu.roll(z_part, 1, 2)
    got(x_low.at[0], 0)
    got(x_low.at[1], 1)
    got(x_high, 2)
    flux = f_x * (here - jnp.concatenate([here[1:], x_high[...][None]], 0))
    edge = x_low[1] * (x_low[0] - here[0])
    x_part = flux - jnp.concatenate([edge[None], flux[:-1]], 0)
    got(y_low, 3)
    got(y_high, 4)
    row = lax.broadcasted_iota(jnp.int32, here.shape, 1)
    above = jnp.where(row == s.Y - 1, y_high[...][:, None, :], pltpu.roll(here, s.Y - 1, 1))
    flux = f_y * (here - above)
    edge = (y_low[1] * (y_low[0] - here[:, 0, :]))[:, None, :]
    y_part = flux - jnp.where(row == 0, edge, pltpu.roll(flux, 1, 1))
    ready(1)
    residual = src[...] - (x_part + y_part + z_part)

    coarse_res = right_exact(left_exact(left[0], residual.reshape(s.X * s.Y, s.Z)), right[0])
    mid, bottom = coarse_res[: s.RM, :LANES], coarse_res[s.RM :, LANES:]
    group = lax.broadcasted_iota(jnp.int32, (s.xb, LANES), 1) // s.zb
    slot = jnp.zeros((s.xb, LANES), jnp.float32)
    for y in range(s.yb):
        slot = slot + jnp.where(
            group == lax.rem(a * s.yb + y, s.per), bottom[y * s.xb : (y + 1) * s.xb], 0.0
        )
    gathered[me] = slot
    each(others, lambda i: put(gathered.at[me], gathered.at[me], 10, shifted(i)))
    for y in range(s.ym):
        plane = mid[y * s.xm : (y + 1) * s.xm]
        res_own[a * s.ym + y] = plane
        res_side_src[0, y] = plane[s.xm - SWEEPS :]
        res_side_src[1, y] = plane[:SWEEPS]
    to_sides(lambda side, to: put(res_side_src.at[side], res_side.at[side, own_rows], 8, to))
    to_members(lambda to: put(res_own.at[own_rows], res_own.at[own_rows], 9, to))

    got(coef_side, 5)
    part = coef_own.at[pl.ds(0, (s.A - 1) * s.ym)]
    got(part, 6)
    got(coef_bot.at[pl.ds(0, (s.S * s.A - 1) * s.yb)], 7)
    mid_faces[...] = jnp.ones(mid_faces.shape, jnp.float32)
    bot_faces[...] = jnp.ones(bot_faces.shape, jnp.float32)
    for d in range(3):
        mid_faces[d, :, 0:SWEEPS, :] = coef_side[0, :, d]
        mid_faces[d, :, SWEEPS : SWEEPS + s.xm, :] = coef_own[:, d]
        mid_faces[d, :, SWEEPS + s.xm : 2 * SWEEPS + s.xm, :] = coef_side[1, :, d]
        for k in range(s.S):
            for y in range(s.YB):
                total = coef_bot[k * s.A * s.yb + y * s.q, d]
                for i in range(1, s.q):
                    total = total + coef_bot[k * s.A * s.yb + y * s.q + i, d]
                bot_faces[d, y, k * s.xb : (k + 1) * s.xb, :] = total

    got(gathered.at[pl.ds(0, others)], 10)
    chunk = s.A // s.NL
    for i in range(s.G):
        for k in range(s.NL):
            total = gathered[i * s.A + k * chunk]
            for j in range(1, chunk):
                total = total + gathered[i * s.A + k * chunk + j]
            bottom_all[i * s.xb : (i + 1) * s.xb, k * LANES : (k + 1) * LANES] = total
    everything = bottom_all[...]
    ready(7, 8, 9, 10, 11, 12, 13, 14)
    modes = right_parts(everything, to_modes[0], to_modes[1])
    modes = full_dot(qx_t[...], modes) * inverse[...]
    near = from_x[g]
    field = right_parts(full_dot(near[:, : s.NXB], modes), from_modes[0], from_modes[1])
    source = right_exact(full_dot(near[:, s.NXB :], everything), spread[...])
    planes = lambda wide: jnp.stack([wide[:, y * LANES : (y + 1) * LANES] for y in range(s.YB)])
    field = sweeps(planes(field), planes(source), [bot_faces[d] for d in range(3)], 0.25**s.merges)

    field = right_exact(field.reshape(s.YB * s.XBP, LANES), grow_z[...])
    field = left_exact(grow_x[...], field).reshape(s.YB, s.XMP, LANES)
    field = jnp.stack([field[y // 2] for y in range(s.YM)])
    got(res_side, 8)
    got(res_own.at[pl.ds(0, (s.A - 1) * s.ym)], 9)
    mid_res[...] = jnp.zeros(mid_res.shape, jnp.float32)
    mid_res[:, 0:SWEEPS, :] = res_side[0]
    mid_res[:, SWEEPS : SWEEPS + s.xm, :] = res_own[...]
    mid_res[:, SWEEPS + s.xm : 2 * SWEEPS + s.xm, :] = res_side[1]
    final[...] = sweeps(field, mid_res[...], [mid_faces[d] for d in range(3)], 0.25 ** (s.merges - 1))
    out[...] = final[own_rows, SWEEPS : SWEEPS + s.xm, : s.zm]

    sent = (
        x_high, x_high, x_high, y_low, y_high, coef_side, part, coef_bot.at[pl.ds(0, (s.S * s.A - 1) * s.yb)],
        res_side, res_own.at[pl.ds(0, (s.A - 1) * s.ym)], gathered.at[pl.ds(0, others)],
    )
    for kind, ref in enumerate(sent):
        got(ref, kind, send)


def local(s, constants, sol, src, fx, fy, fz):
    f32 = lambda *shape: pltpu.VMEM(shape, jnp.float32)
    total = s.G * s.A
    arrays = (sol, src, fx, fy, fz, *constants)
    result = pl.pallas_call(
        functools.partial(kernel, s, len(arrays)),
        out_shape=jax.ShapeDtypeStruct((s.ym, s.xm, s.zm), jnp.float32),
        in_specs=[pl.BlockSpec(memory_space=pltpu.HBM)] * len(arrays),
        out_specs=pl.BlockSpec(memory_space=pltpu.VMEM),
        scratch_shapes=[
            *[pltpu.VMEM(array.shape, array.dtype) for array in arrays],
            f32(2, s.Y, s.Z), f32(s.Y, s.Z), f32(2, s.X, s.Z), f32(s.X, s.Z), f32(2, s.X, s.Z), f32(s.X, s.Z),
            f32(s.YM, 3, s.xm, LANES), f32(2, s.YM, 3, SWEEPS, LANES), f32(2, s.ym, 3, SWEEPS, LANES),
            f32(s.S * s.A * s.yb, 3, s.xb, LANES),
            f32(s.YM, s.xm, LANES), f32(2, s.YM, SWEEPS, LANES), f32(2, s.ym, SWEEPS, LANES),
            f32(total, s.xb, LANES),
            f32(s.NXB, s.NL * LANES), f32(3, s.YM, s.XMP, LANES), f32(s.YM, s.XMP, LANES),
            f32(3, s.YB, s.XBP, LANES), f32(s.YM, s.XMP, LANES),
            pltpu.SemaphoreType.DMA((11,)),
            pltpu.SemaphoreType.DMA((11,)),
            pltpu.SemaphoreType.DMA((len(arrays),)),
        ],
        compiler_params=pltpu.CompilerParams(
            collective_id=0, has_side_effects=True, vmem_limit_bytes=32 * 1024 * 1024
        ),
    )(*arrays)
    return jnp.transpose(result, (1, 0, 2))


def solution(mesh):
    groups, members = mesh.shape["grp"], mesh.shape["agg"]

    def whole(*arrays):
        nx, ny, nz = arrays[0].shape
        s = Sizes(groups, members, (nx // groups, ny // members, nz))
        constants = [jnp.asarray(t) for t in tables(s)]
        return jax.shard_map(
            functools.partial(local, s, constants),
            mesh=mesh,
            in_specs=(P("grp", "agg", None),) * 5,
            out_specs=P("grp", "agg", None),
            check_vma=False,
        )(*arrays)

    return whole
```

```python
import functools

import jax
import jax.numpy as jnp
import ml_dtypes
import numpy as np
from jax import lax
from jax.experimental import pallas as pl
from jax.experimental.pallas import tpu as pltpu
from jax.sharding import PartitionSpec as P

LANES = 128
SWEEPS = 2
MESH = pl.DeviceIdType.MESH


class Sizes:
    def __init__(self, groups, members, block):
        self.G, self.A = groups, members
        self.X, self.Y, self.Z = block
        self.merges = members.bit_length() - 1
        self.f = 2 ** (self.merges - 1)
        self.b = 2**self.merges
        self.xm, self.ym, self.zm = self.X // self.f, self.Y // self.f, self.Z // self.f
        self.xb, self.zb = self.X // self.b, self.Z // self.b
        self.yb = max(1, self.Y // self.b)
        self.YM, self.YB = self.A * self.ym, self.A * self.Y // self.b
        self.q = self.A * self.yb // self.YB
        self.h = -(-(SWEEPS + 1) // self.xb)
        self.S = 2 * self.h + 1
        self.NXB = self.G * self.xb
        self.XBP = -(-self.S * self.xb // 8) * 8
        self.XMP = -(-(self.xm + 2 * SWEEPS) // 8) * 8
        self.RM = -(-self.ym * self.xm // 8) * 8
        self.RB = -(-self.yb * self.xb // 8) * 8
        self.per = LANES // self.zb
        self.NL = self.A * self.yb * self.zb // LANES


def bf16_parts(table):
    first = table.astype(ml_dtypes.bfloat16)
    second = (table - first.astype(np.float64)).astype(ml_dtypes.bfloat16)
    return np.stack([first, second])


def real_basis(count):
    at = np.arange(count)[:, None]
    mode = np.arange(count)
    wave = (mode + 1) // 2
    angle = 2 * np.pi * ((at * wave[None, :]) % count) / count
    basis = np.where(mode[None, :] % 2 == 1, np.cos(angle), np.sin(angle)) * np.sqrt(2.0 / count)
    basis[:, 0] = np.sqrt(1.0 / count)
    if count % 2 == 0:
        basis[:, count - 1] = np.sqrt(1.0 / count) * (1 - 2 * (np.arange(count) % 2))
    return basis, wave


def tables(s):
    left = np.zeros((4, s.RM + s.RB, s.X * s.Y))
    for x in range(s.X):
        for y in range(s.Y):
            for base, f, xn, in ((0, s.f, s.xm), (s.RM, s.b, s.xb)):
                row, col = base + (y // f) * xn + x // f, x * s.Y + y
                last_x, last_y = x % f == f - 1, y % f == f - 1 or (f > s.Y and y == s.Y - 1)
                left[0, row, col] = 1 / f**2
                left[1, row, col] = last_x / f
                left[2, row, col] = last_y / f
                left[3, row, col] = 1 / f**2
    right = np.zeros((2, s.Z, 2 * LANES))
    for lane in range(LANES):
        for base, f, zn in ((0, s.f, s.zm), (LANES, s.b, s.zb)):
            z = lane % zn
            right[0, z * f : (z + 1) * f, base + lane] = 1 / f
            right[1, (z + 1) * f - 1, base + lane] = 1
    qx, wx = real_basis(s.NXB)
    qy, wy = real_basis(s.YB)
    qz, wz = real_basis(s.zb)
    rows = np.arange(s.A * s.yb) // s.q
    to_modes = np.einsum("yk,zl->yzkl", qy[rows], qz).reshape(s.NL * LANES, s.YB * s.zb)
    copies = np.arange(LANES) % s.zb
    from_modes = np.einsum("yk,zl->klyz", qy, qz[copies]).reshape(s.YB * s.zb, s.YB * LANES)
    spread = np.einsum("ay,zl->azyl", rows[:, None] == np.arange(s.YB), np.arange(s.zb)[:, None] == copies[None, :])
    spread = spread.reshape(s.NL * LANES, s.YB * LANES).astype(np.float64)

    def eigen(wave, count):
        return 2.0 - 2.0 * np.cos(2.0 * np.pi * wave / count)

    symbol = (
        eigen(wx, s.NXB)[:, None, None] + eigen(wy, s.YB)[None, :, None] + eigen(wz, s.zb)[None, None, :]
    ).reshape(s.NXB, -1) * 0.25**s.merges
    symbol[0, 0] = 1.0
    inverse = 1.0 / symbol
    inverse[0, 0] = 0.0
    near = (np.arange(s.G)[:, None] * s.xb - s.h * s.xb + np.arange(s.XBP)[None, :]) % s.NXB
    qx_near = qx[near]
    pick = (near[:, :, None] == np.arange(s.NXB)).astype(np.float32)
    from_x = np.concatenate([qx_near, pick], 2).astype(np.float32)
    grow_x = np.zeros((s.XMP, s.XBP))
    for row in range(s.XMP):
        grow_x[row, min(s.h * s.xb + (row - SWEEPS) // 2, s.XBP - 1)] = 1
    grow_x = np.kron(np.eye(s.YB), grow_x)
    grow_z = np.zeros((LANES, LANES))
    for lane in range(LANES):
        grow_z[(lane % s.zm) // 2, lane] = 1
    bf = lambda t: t.astype(ml_dtypes.bfloat16)
    return (
        bf(left), bf(right), bf16_parts(to_modes), bf16_parts(from_modes), bf(spread),
        qx.T.astype(np.float32), inverse.astype(np.float32), from_x, bf(grow_x), bf(grow_z),
    )


def cut(value, count):
    parts = []
    for _ in range(count):
        part = value.astype(jnp.bfloat16).astype(jnp.float32)
        parts.append(part)
        value = value - part
    return parts


def dot(one, two):
    return jnp.dot(one, two, preferred_element_type=jnp.float32)


def right_exact(value, table, count=3):
    rows = value.shape[0]
    product = dot(jnp.concatenate(cut(value, count), 0).astype(jnp.bfloat16), table)
    return sum(product[i * rows : (i + 1) * rows] for i in reversed(range(count)))


def left_exact(table, value, count=3):
    columns = value.shape[1]
    product = dot(table, jnp.concatenate(cut(value, count), 1).astype(jnp.bfloat16))
    return sum(product[:, i * columns : (i + 1) * columns] for i in reversed(range(count)))


def right_parts(value, high, low):
    rows = value.shape[0]
    stacked = jnp.concatenate(cut(value, 2), 0).astype(jnp.bfloat16)
    by_high = dot(stacked, high)
    by_low = dot(stacked, low)
    return by_low[:rows] + by_high[rows:] + by_low[rows:] + by_high[:rows]


def full_dot(one, two):
    return jnp.dot(one, two, precision=lax.Precision.HIGHEST, preferred_element_type=jnp.float32)


def turned(value, step, axis):
    if axis == 0:
        return jnp.concatenate([value[step:], value[:step]], 0)
    return pltpu.roll(value, (-step) % value.shape[axis], axis)


def sweeps(current, residual, faces, factor):
    along = (1, 0, 2)
    below = [turned(face, -1, d) for face, d in zip(faces, along)]
    diagonal = sum(face + under for face, under in zip(faces, below))
    scale = (2.0 / 3.0) / (factor * diagonal)
    for _ in range(SWEEPS):
        applied = diagonal * current
        for face, under, d in zip(faces, below, along):
            applied = applied - face * turned(current, 1, d) - under * turned(current, -1, d)
        current = current + scale * (residual - factor * applied)
    return current


def each(count, body):
    if count <= 64:
        for i in range(count):
            body(i)
    else:
        lax.fori_loop(0, count, lambda i, c: (body(i), c)[1], 0)


def kernel(
    s, operand_count, *refs
):
    operands, out, held = refs[:operand_count], refs[operand_count], refs[operand_count + 1 : 2 * operand_count + 1]
    body(s, operands, out, held, *refs[2 * operand_count + 1 :])


def body(
    s, operands, out, held,
    x_low, x_high, y_low, y_high, y_low_src, y_high_src,
    coef_own, coef_side, coef_side_src, coef_bot,
    res_own, res_side, res_side_src, gathered,
    bottom_all, mid_faces, mid_res, bot_faces, final,
    send, recv, loaded,
):
    sol, src, fx, fy, fz, left, right, to_modes, from_modes, spread, qx_t, inverse, from_x, grow_x, grow_z = held
    g, a = lax.axis_index("grp"), lax.axis_index("agg")
    me = g * s.A + a
    others = s.G * s.A - 1

    def shifted(i):
        at = lax.rem(me + 1 + i, s.G * s.A)
        return {"grp": at // s.A, "agg": lax.rem(at, s.A)}

    barrier = pltpu.get_barrier_semaphore()
    each(others, lambda i: pl.semaphore_signal(barrier, inc=1, device_id=shifted(i), device_id_type=MESH))

    order = (0, 3, 2, 4, 5, 6, 1, 7, 10, 11, 12, 8, 9, 13, 14)
    loads = [pltpu.make_async_copy(operands[i], held[i], loaded.at[i]) for i in range(len(held))]
    for i in order:
        loads[i].start()

    def ready(*which):
        for i in which:
            loads[i].wait()

    ready(0, 3)
    y_low_src[0] = sol[:, s.Y - 1, :]
    y_low_src[1] = fy[:, s.Y - 1, :]
    y_high_src[...] = sol[:, 0, :]

    def put(src_ref, dst_ref, kind, to):
        copy = pltpu.make_async_remote_copy(
            src_ref=src_ref, dst_ref=dst_ref, send_sem=send.at[kind], recv_sem=recv.at[kind],
            device_id=to, device_id_type=MESH,
        )
        copy.start()

    up, down = lax.rem(g + 1, s.G), lax.rem(g + s.G - 1, s.G)
    right_of, left_of = lax.rem(a + 1, s.A), lax.rem(a + s.A - 1, s.A)

    ready(2)
    pl.semaphore_wait(barrier, others)
    put(sol.at[s.X - 1], x_low.at[0], 0, {"grp": up, "agg": a})
    put(fx.at[s.X - 1], x_low.at[1], 1, {"grp": up, "agg": a})
    put(sol.at[0], x_high, 2, {"grp": down, "agg": a})
    put(y_low_src, y_low, 3, {"grp": g, "agg": right_of})
    put(y_high_src, y_high, 4, {"grp": g, "agg": left_of})

    ready(4, 5, 6)
    flat = lambda ref: ref[...].reshape(s.X * s.Y, s.Z)
    half = s.RM + s.RB
    rows = [left_exact(left[d + 1], flat(ref)) for d, ref in enumerate((fx, fy, fz))]
    both = right_exact(jnp.concatenate(rows[:2], 0), right[0])
    coarse = [both[:half], both[half:], right_exact(rows[2], right[1])]
    for d in range(3):
        mid, bottom = coarse[d][: s.RM, :LANES], coarse[d][s.RM :, LANES:]
        if d == 1 and s.q > 1:
            bottom = jnp.where(lax.rem(a, s.q) == s.q - 1, bottom, 0.0)
        for y in range(s.ym):
            plane = mid[y * s.xm : (y + 1) * s.xm]
            coef_own[a * s.ym + y, d] = plane
            coef_side_src[0, y, d] = plane[s.xm - SWEEPS :]
            coef_side_src[1, y, d] = plane[:SWEEPS]
        for y in range(s.yb):
            coef_bot[(s.h * s.A + a) * s.yb + y, d] = bottom[y * s.xb : (y + 1) * s.xb]

    own_rows = pl.ds(a * s.ym, s.ym)
    bot_rows = lambda k: pl.ds((k * s.A + a) * s.yb, s.yb)

    def to_members(body):
        each(s.A - 1, lambda i: body({"grp": g, "agg": lax.rem(a + 1 + i, s.A)}))

    def to_sides(body):
        for side, to in ((0, up), (1, down)):
            each(s.A, lambda i: body(side, {"grp": to, "agg": lax.rem(a + i, s.A)}))

    to_sides(lambda side, to: put(coef_side_src.at[side], coef_side.at[side, own_rows], 5, to))
    to_members(lambda to: put(coef_own.at[own_rows], coef_own.at[own_rows], 6, to))
    bot_src = coef_bot.at[bot_rows(s.h)]
    for d in range(-s.h, s.h + 1):
        to_g = lax.rem(g + d + s.G, s.G)
        send_bot = lambda to: put(bot_src, coef_bot.at[bot_rows(s.h - d)], 7, to)
        if d == 0:
            to_members(send_bot)
        else:
            each(s.A, lambda i: send_bot({"grp": to_g, "agg": lax.rem(a + i, s.A)}))

    def got(ref, kind, sems=recv):
        pltpu.make_async_copy(ref, ref, sems.at[kind]).wait()

    here = sol[...]
    f_x, f_y, f_z = fx[...], fy[...], fz[...]
    z_part = f_z * (here - pltpu.roll(here, s.Z - 1, 2))
    z_part = z_part - pltpu.roll(z_part, 1, 2)
    got(x_low.at[0], 0)
    got(x_low.at[1], 1)
    got(x_high, 2)
    flux = f_x * (here - jnp.concatenate([here[1:], x_high[...][None]], 0))
    edge = x_low[1] * (x_low[0] - here[0])
    x_part = flux - jnp.concatenate([edge[None], flux[:-1]], 0)
    got(y_low, 3)
    got(y_high, 4)
    row = lax.broadcasted_iota(jnp.int32, here.shape, 1)
    above = jnp.where(row == s.Y - 1, y_high[...][:, None, :], pltpu.roll(here, s.Y - 1, 1))
    flux = f_y * (here - above)
    edge = (y_low[1] * (y_low[0] - here[:, 0, :]))[:, None, :]
    y_part = flux - jnp.where(row == 0, edge, pltpu.roll(flux, 1, 1))
    ready(1)
    residual = src[...] - (x_part + y_part + z_part)

    coarse_res = right_exact(left_exact(left[0], residual.reshape(s.X * s.Y, s.Z)), right[0])
    mid, bottom = coarse_res[: s.RM, :LANES], coarse_res[s.RM :, LANES:]
    group = lax.broadcasted_iota(jnp.int32, (s.xb, LANES), 1) // s.zb
    slot = jnp.zeros((s.xb, LANES), jnp.float32)
    for y in range(s.yb):
        slot = slot + jnp.where(
            group == lax.rem(a * s.yb + y, s.per), bottom[y * s.xb : (y + 1) * s.xb], 0.0
        )
    gathered[me] = slot
    each(others, lambda i: put(gathered.at[me], gathered.at[me], 10, shifted(i)))
    for y in range(s.ym):
        plane = mid[y * s.xm : (y + 1) * s.xm]
        res_own[a * s.ym + y] = plane
        res_side_src[0, y] = plane[s.xm - SWEEPS :]
        res_side_src[1, y] = plane[:SWEEPS]
    to_sides(lambda side, to: put(res_side_src.at[side], res_side.at[side, own_rows], 8, to))
    to_members(lambda to: put(res_own.at[own_rows], res_own.at[own_rows], 9, to))

    got(coef_side, 5)
    part = coef_own.at[pl.ds(0, (s.A - 1) * s.ym)]
    got(part, 6)
    got(coef_bot.at[pl.ds(0, (s.S * s.A - 1) * s.yb)], 7)
    mid_faces[...] = jnp.ones(mid_faces.shape, jnp.float32)
    bot_faces[...] = jnp.ones(bot_faces.shape, jnp.float32)
    for d in range(3):
        mid_faces[d, :, 0:SWEEPS, :] = coef_side[0, :, d]
        mid_faces[d, :, SWEEPS : SWEEPS + s.xm, :] = coef_own[:, d]
        mid_faces[d, :, SWEEPS + s.xm : 2 * SWEEPS + s.xm, :] = coef_side[1, :, d]
        for k in range(s.S):
            for y in range(s.YB):
                total = coef_bot[k * s.A * s.yb + y * s.q, d]
                for i in range(1, s.q):
                    total = total + coef_bot[k * s.A * s.yb + y * s.q + i, d]
                bot_faces[d, y, k * s.xb : (k + 1) * s.xb, :] = total

    got(gathered.at[pl.ds(0, others)], 10)
    chunk = s.A // s.NL
    for i in range(s.G):
        for k in range(s.NL):
            total = gathered[i * s.A + k * chunk]
            for j in range(1, chunk):
                total = total + gathered[i * s.A + k * chunk + j]
            bottom_all[i * s.xb : (i + 1) * s.xb, k * LANES : (k + 1) * LANES] = total
    everything = bottom_all[...]
    ready(7, 8, 9, 10, 11, 12, 13, 14)
    modes = right_parts(everything, to_modes[0], to_modes[1])
    modes = full_dot(qx_t[...], modes) * inverse[...]
    near = from_x[g]
    field = right_parts(full_dot(near[:, : s.NXB], modes), from_modes[0], from_modes[1])
    source = right_exact(full_dot(near[:, s.NXB :], everything), spread[...])
    planes = lambda wide: jnp.stack([wide[:, y * LANES : (y + 1) * LANES] for y in range(s.YB)])
    field = sweeps(planes(field), planes(source), [bot_faces[d] for d in range(3)], 0.25**s.merges)

    field = right_exact(field.reshape(s.YB * s.XBP, LANES), grow_z[...])
    field = left_exact(grow_x[...], field).reshape(s.YB, s.XMP, LANES)
    field = jnp.stack([field[y // 2] for y in range(s.YM)])
    got(res_side, 8)
    got(res_own.at[pl.ds(0, (s.A - 1) * s.ym)], 9)
    mid_res[...] = jnp.zeros(mid_res.shape, jnp.float32)
    mid_res[:, 0:SWEEPS, :] = res_side[0]
    mid_res[:, SWEEPS : SWEEPS + s.xm, :] = res_own[...]
    mid_res[:, SWEEPS + s.xm : 2 * SWEEPS + s.xm, :] = res_side[1]
    final[...] = sweeps(field, mid_res[...], [mid_faces[d] for d in range(3)], 0.25 ** (s.merges - 1))
    out[...] = final[own_rows, SWEEPS : SWEEPS + s.xm, : s.zm]

    sent = (
        x_high, x_high, x_high, y_low, y_high, coef_side, part, coef_bot.at[pl.ds(0, (s.S * s.A - 1) * s.yb)],
        res_side, res_own.at[pl.ds(0, (s.A - 1) * s.ym)], gathered.at[pl.ds(0, others)],
    )
    for kind, ref in enumerate(sent):
        got(ref, kind, send)


def local(s, constants, sol, src, fx, fy, fz):
    f32 = lambda *shape: pltpu.VMEM(shape, jnp.float32)
    total = s.G * s.A
    arrays = (sol, src, fx, fy, fz, *constants)
    result = pl.pallas_call(
        functools.partial(kernel, s, len(arrays)),
        out_shape=jax.ShapeDtypeStruct((s.ym, s.xm, s.zm), jnp.float32),
        in_specs=[pl.BlockSpec(memory_space=pltpu.HBM)] * len(arrays),
        out_specs=pl.BlockSpec(memory_space=pltpu.VMEM),
        scratch_shapes=[
            *[pltpu.VMEM(array.shape, array.dtype) for array in arrays],
            f32(2, s.Y, s.Z), f32(s.Y, s.Z), f32(2, s.X, s.Z), f32(s.X, s.Z), f32(2, s.X, s.Z), f32(s.X, s.Z),
            f32(s.YM, 3, s.xm, LANES), f32(2, s.YM, 3, SWEEPS, LANES), f32(2, s.ym, 3, SWEEPS, LANES),
            f32(s.S * s.A * s.yb, 3, s.xb, LANES),
            f32(s.YM, s.xm, LANES), f32(2, s.YM, SWEEPS, LANES), f32(2, s.ym, SWEEPS, LANES),
            f32(total, s.xb, LANES),
            f32(s.NXB, s.NL * LANES), f32(3, s.YM, s.XMP, LANES), f32(s.YM, s.XMP, LANES),
            f32(3, s.YB, s.XBP, LANES), f32(s.YM, s.XMP, LANES),
            pltpu.SemaphoreType.DMA((11,)),
            pltpu.SemaphoreType.DMA((11,)),
            pltpu.SemaphoreType.DMA((len(arrays),)),
        ],
        compiler_params=pltpu.CompilerParams(
            collective_id=0, has_side_effects=True
        ),
    )(*arrays)
    return jnp.transpose(result, (1, 0, 2))


def solution(mesh):
    groups, members = mesh.shape["grp"], mesh.shape["agg"]

    def whole(*arrays):
        nx, ny, nz = arrays[0].shape
        s = Sizes(groups, members, (nx // groups, ny // members, nz))
        constants = [jnp.asarray(t) for t in tables(s)]
        return jax.shard_map(
            functools.partial(local, s, constants),
            mesh=mesh,
            in_specs=(P("grp", "agg", None),) * 5,
            out_specs=P("grp", "agg", None),
            check_vma=False,
        )(*arrays)

    return whole
```

```python
import functools

import jax
import jax.numpy as jnp
import ml_dtypes
import numpy as np
from jax import lax
from jax.experimental import pallas as pl
from jax.experimental.pallas import tpu as pltpu
from jax.sharding import PartitionSpec as P

LANES = 128
SWEEPS = 2
MESH = pl.DeviceIdType.MESH


class Sizes:
    def __init__(self, groups, members, block):
        self.G, self.A = groups, members
        self.X, self.Y, self.Z = block
        self.merges = members.bit_length() - 1
        self.f = 2 ** (self.merges - 1)
        self.b = 2**self.merges
        self.xm, self.ym, self.zm = self.X // self.f, self.Y // self.f, self.Z // self.f
        self.xb, self.zb = self.X // self.b, self.Z // self.b
        self.yb = max(1, self.Y // self.b)
        self.YM, self.YB = self.A * self.ym, self.A * self.Y // self.b
        self.q = self.A * self.yb // self.YB
        self.h = -(-(SWEEPS + 1) // self.xb)
        self.S = 2 * self.h + 1
        self.NXB = self.G * self.xb
        self.XBP = -(-self.S * self.xb // 8) * 8
        self.XMP = -(-(self.xm + 2 * SWEEPS) // 8) * 8
        self.RM = -(-self.ym * self.xm // 8) * 8
        self.RB = -(-self.yb * self.xb // 8) * 8
        self.per = LANES // self.zb
        self.NL = self.A * self.yb * self.zb // LANES


def bf16_parts(table):
    first = table.astype(ml_dtypes.bfloat16)
    second = (table - first.astype(np.float64)).astype(ml_dtypes.bfloat16)
    return np.stack([first, second])


def real_basis(count):
    at = np.arange(count)[:, None]
    mode = np.arange(count)
    wave = (mode + 1) // 2
    angle = 2 * np.pi * ((at * wave[None, :]) % count) / count
    basis = np.where(mode[None, :] % 2 == 1, np.cos(angle), np.sin(angle)) * np.sqrt(2.0 / count)
    basis[:, 0] = np.sqrt(1.0 / count)
    if count % 2 == 0:
        basis[:, count - 1] = np.sqrt(1.0 / count) * (1 - 2 * (np.arange(count) % 2))
    return basis, wave


def tables(s):
    left = np.zeros((4, s.RM + s.RB, s.X * s.Y))
    for x in range(s.X):
        for y in range(s.Y):
            for base, f, xn, in ((0, s.f, s.xm), (s.RM, s.b, s.xb)):
                row, col = base + (y // f) * xn + x // f, x * s.Y + y
                last_x, last_y = x % f == f - 1, y % f == f - 1 or (f > s.Y and y == s.Y - 1)
                left[0, row, col] = 1 / f**2
                left[1, row, col] = last_x / f
                left[2, row, col] = last_y / f
                left[3, row, col] = 1 / f**2
    right = np.zeros((2, s.Z, 2 * LANES))
    for lane in range(LANES):
        for base, f, zn in ((0, s.f, s.zm), (LANES, s.b, s.zb)):
            z = lane % zn
            right[0, z * f : (z + 1) * f, base + lane] = 1 / f
            right[1, (z + 1) * f - 1, base + lane] = 1
    qx, wx = real_basis(s.NXB)
    qy, wy = real_basis(s.YB)
    qz, wz = real_basis(s.zb)
    rows = np.arange(s.A * s.yb) // s.q
    to_modes = np.einsum("yk,zl->yzkl", qy[rows], qz).reshape(s.NL * LANES, s.YB * s.zb)
    copies = np.arange(LANES) % s.zb
    from_modes = np.einsum("yk,zl->klyz", qy, qz[copies]).reshape(s.YB * s.zb, s.YB * LANES)
    spread = np.einsum("ay,zl->azyl", rows[:, None] == np.arange(s.YB), np.arange(s.zb)[:, None] == copies[None, :])
    spread = spread.reshape(s.NL * LANES, s.YB * LANES).astype(np.float64)

    def eigen(wave, count):
        return 2.0 - 2.0 * np.cos(2.0 * np.pi * wave / count)

    symbol = (
        eigen(wx, s.NXB)[:, None, None] + eigen(wy, s.YB)[None, :, None] + eigen(wz, s.zb)[None, None, :]
    ).reshape(s.NXB, -1) * 0.25**s.merges
    symbol[0, 0] = 1.0
    inverse = 1.0 / symbol
    inverse[0, 0] = 0.0
    near = (np.arange(s.G)[:, None] * s.xb - s.h * s.xb + np.arange(s.XBP)[None, :]) % s.NXB
    qx_near = qx[near]
    pick = (near[:, :, None] == np.arange(s.NXB)).astype(np.float32)
    from_x = np.concatenate([qx_near, pick], 2).astype(np.float32)
    grow_x = np.zeros((s.XMP, s.XBP))
    for row in range(s.XMP):
        grow_x[row, min(s.h * s.xb + (row - SWEEPS) // 2, s.XBP - 1)] = 1
    grow_x = np.kron(np.eye(s.YB), grow_x)
    grow_z = np.zeros((LANES, LANES))
    for lane in range(LANES):
        grow_z[(lane % s.zm) // 2, lane] = 1
    bf = lambda t: t.astype(ml_dtypes.bfloat16)
    return (
        bf(left), bf(right), bf16_parts(to_modes), bf16_parts(from_modes), bf(spread),
        qx.T.astype(np.float32), inverse.astype(np.float32), from_x, bf(grow_x), bf(grow_z),
    )


def cut(value, count):
    parts = []
    for _ in range(count):
        part = value.astype(jnp.bfloat16).astype(jnp.float32)
        parts.append(part)
        value = value - part
    return parts


def dot(one, two):
    return jnp.dot(one, two, preferred_element_type=jnp.float32)


def right_exact(value, table, count=3):
    rows = value.shape[0]
    product = dot(jnp.concatenate(cut(value, count), 0).astype(jnp.bfloat16), table)
    return sum(product[i * rows : (i + 1) * rows] for i in reversed(range(count)))


def left_exact(table, value, count=3):
    columns = value.shape[1]
    product = dot(table, jnp.concatenate(cut(value, count), 1).astype(jnp.bfloat16))
    return sum(product[:, i * columns : (i + 1) * columns] for i in reversed(range(count)))


def right_parts(value, high, low):
    rows = value.shape[0]
    stacked = jnp.concatenate(cut(value, 2), 0).astype(jnp.bfloat16)
    by_high = dot(stacked, high)
    by_low = dot(stacked, low)
    return by_low[:rows] + by_high[rows:] + by_low[rows:] + by_high[:rows]


def full_dot(one, two):
    return jnp.dot(one, two, precision=lax.Precision.HIGHEST, preferred_element_type=jnp.float32)


def turned(value, step, axis):
    if axis == 0:
        return jnp.concatenate([value[step:], value[:step]], 0)
    return pltpu.roll(value, (-step) % value.shape[axis], axis)


def sweeps(current, residual, faces, factor):
    along = (1, 0, 2)
    below = [turned(face, -1, d) for face, d in zip(faces, along)]
    diagonal = sum(face + under for face, under in zip(faces, below))
    scale = (2.0 / 3.0) / (factor * diagonal)
    for _ in range(SWEEPS):
        applied = diagonal * current
        for face, under, d in zip(faces, below, along):
            applied = applied - face * turned(current, 1, d) - under * turned(current, -1, d)
        current = current + scale * (residual - factor * applied)
    return current


def each(count, body):
    if count <= 64:
        for i in range(count):
            body(i)
    else:
        lax.fori_loop(0, count, lambda i, c: (body(i), c)[1], 0)


def kernel(
    s, operand_count, *refs
):
    operands, out, held = refs[:operand_count], refs[operand_count], refs[operand_count + 1 : 2 * operand_count + 1]
    body(s, operands, out, held, *refs[2 * operand_count + 1 :])


def body(
    s, operands, out, held,
    x_low, x_high, y_low, y_high, y_low_src, y_high_src,
    coef_own, coef_side, coef_side_src, coef_bot,
    res_own, res_side, res_side_src, gathered,
    bottom_all, mid_faces, mid_res, bot_faces, final,
    send, recv, loaded,
):
    sol, src, fx, fy, fz, left, right, to_modes, from_modes, spread, qx_t, inverse, from_x, grow_x, grow_z = held
    g, a = lax.axis_index("grp"), lax.axis_index("agg")
    me = g * s.A + a
    others = s.G * s.A - 1

    def shifted(i):
        at = lax.rem(me + 1 + i, s.G * s.A)
        return {"grp": at // s.A, "agg": lax.rem(at, s.A)}

    order = (0, 3, 2, 4, 5, 6, 1, 7, 10, 11, 12, 8, 9, 13, 14)
    loads = [pltpu.make_async_copy(operands[i], held[i], loaded.at[i]) for i in range(len(held))]
    for i in order:
        loads[i].start()
    barrier = pltpu.get_barrier_semaphore()
    each(others, lambda i: pl.semaphore_signal(barrier, inc=1, device_id=shifted(i), device_id_type=MESH))

    def ready(*which):
        for i in which:
            loads[i].wait()

    ready(0, 3)
    y_low_src[0] = sol[:, s.Y - 1, :]
    y_low_src[1] = fy[:, s.Y - 1, :]
    y_high_src[...] = sol[:, 0, :]

    ready(2, 4, 5, 6)
    flat = lambda ref: ref[...].reshape(s.X * s.Y, s.Z)
    half = s.RM + s.RB
    rows = [left_exact(left[d + 1], flat(ref)) for d, ref in enumerate((fx, fy, fz))]
    both = right_exact(jnp.concatenate(rows[:2], 0), right[0])
    coarse = [both[:half], both[half:], right_exact(rows[2], right[1])]
    for d in range(3):
        mid, bottom = coarse[d][: s.RM, :LANES], coarse[d][s.RM :, LANES:]
        if d == 1 and s.q > 1:
            bottom = jnp.where(lax.rem(a, s.q) == s.q - 1, bottom, 0.0)
        for y in range(s.ym):
            plane = mid[y * s.xm : (y + 1) * s.xm]
            coef_own[a * s.ym + y, d] = plane
            coef_side_src[0, y, d] = plane[s.xm - SWEEPS :]
            coef_side_src[1, y, d] = plane[:SWEEPS]
        for y in range(s.yb):
            coef_bot[(s.h * s.A + a) * s.yb + y, d] = bottom[y * s.xb : (y + 1) * s.xb]

    def put(src_ref, dst_ref, kind, to):
        copy = pltpu.make_async_remote_copy(
            src_ref=src_ref, dst_ref=dst_ref, send_sem=send.at[kind], recv_sem=recv.at[kind],
            device_id=to, device_id_type=MESH,
        )
        copy.start()

    up, down = lax.rem(g + 1, s.G), lax.rem(g + s.G - 1, s.G)
    right_of, left_of = lax.rem(a + 1, s.A), lax.rem(a + s.A - 1, s.A)

    pl.semaphore_wait(barrier, others)
    put(sol.at[s.X - 1], x_low.at[0], 0, {"grp": up, "agg": a})
    put(fx.at[s.X - 1], x_low.at[1], 1, {"grp": up, "agg": a})
    put(sol.at[0], x_high, 2, {"grp": down, "agg": a})
    put(y_low_src, y_low, 3, {"grp": g, "agg": right_of})
    put(y_high_src, y_high, 4, {"grp": g, "agg": left_of})

    own_rows = pl.ds(a * s.ym, s.ym)
    bot_rows = lambda k: pl.ds((k * s.A + a) * s.yb, s.yb)

    def to_members(body):
        each(s.A - 1, lambda i: body({"grp": g, "agg": lax.rem(a + 1 + i, s.A)}))

    def to_sides(body):
        for side, to in ((0, up), (1, down)):
            each(s.A, lambda i: body(side, {"grp": to, "agg": lax.rem(a + i, s.A)}))

    to_sides(lambda side, to: put(coef_side_src.at[side], coef_side.at[side, own_rows], 5, to))
    to_members(lambda to: put(coef_own.at[own_rows], coef_own.at[own_rows], 6, to))
    bot_src = coef_bot.at[bot_rows(s.h)]
    for d in range(-s.h, s.h + 1):
        to_g = lax.rem(g + d + s.G, s.G)
        send_bot = lambda to: put(bot_src, coef_bot.at[bot_rows(s.h - d)], 7, to)
        if d == 0:
            to_members(send_bot)
        else:
            each(s.A, lambda i: send_bot({"grp": to_g, "agg": lax.rem(a + i, s.A)}))

    def got(ref, kind, sems=recv):
        pltpu.make_async_copy(ref, ref, sems.at[kind]).wait()

    here = sol[...]
    f_x, f_y, f_z = fx[...], fy[...], fz[...]
    z_part = f_z * (here - pltpu.roll(here, s.Z - 1, 2))
    z_part = z_part - pltpu.roll(z_part, 1, 2)
    got(x_low.at[0], 0)
    got(x_low.at[1], 1)
    got(x_high, 2)
    flux = f_x * (here - jnp.concatenate([here[1:], x_high[...][None]], 0))
    edge = x_low[1] * (x_low[0] - here[0])
    x_part = flux - jnp.concatenate([edge[None], flux[:-1]], 0)
    got(y_low, 3)
    got(y_high, 4)
    row = lax.broadcasted_iota(jnp.int32, here.shape, 1)
    above = jnp.where(row == s.Y - 1, y_high[...][:, None, :], pltpu.roll(here, s.Y - 1, 1))
    flux = f_y * (here - above)
    edge = (y_low[1] * (y_low[0] - here[:, 0, :]))[:, None, :]
    y_part = flux - jnp.where(row == 0, edge, pltpu.roll(flux, 1, 1))
    ready(1)
    residual = src[...] - (x_part + y_part + z_part)

    coarse_res = right_exact(left_exact(left[0], residual.reshape(s.X * s.Y, s.Z)), right[0])
    mid, bottom = coarse_res[: s.RM, :LANES], coarse_res[s.RM :, LANES:]
    group = lax.broadcasted_iota(jnp.int32, (s.xb, LANES), 1) // s.zb
    slot = jnp.zeros((s.xb, LANES), jnp.float32)
    for y in range(s.yb):
        slot = slot + jnp.where(
            group == lax.rem(a * s.yb + y, s.per), bottom[y * s.xb : (y + 1) * s.xb], 0.0
        )
    gathered[me] = slot
    each(others, lambda i: put(gathered.at[me], gathered.at[me], 10, shifted(i)))
    for y in range(s.ym):
        plane = mid[y * s.xm : (y + 1) * s.xm]
        res_own[a * s.ym + y] = plane
        res_side_src[0, y] = plane[s.xm - SWEEPS :]
        res_side_src[1, y] = plane[:SWEEPS]
    to_sides(lambda side, to: put(res_side_src.at[side], res_side.at[side, own_rows], 8, to))
    to_members(lambda to: put(res_own.at[own_rows], res_own.at[own_rows], 9, to))

    got(coef_side, 5)
    part = coef_own.at[pl.ds(0, (s.A - 1) * s.ym)]
    got(part, 6)
    got(coef_bot.at[pl.ds(0, (s.S * s.A - 1) * s.yb)], 7)
    mid_faces[...] = jnp.ones(mid_faces.shape, jnp.float32)
    bot_faces[...] = jnp.ones(bot_faces.shape, jnp.float32)
    for d in range(3):
        mid_faces[d, :, 0:SWEEPS, :] = coef_side[0, :, d]
        mid_faces[d, :, SWEEPS : SWEEPS + s.xm, :] = coef_own[:, d]
        mid_faces[d, :, SWEEPS + s.xm : 2 * SWEEPS + s.xm, :] = coef_side[1, :, d]
        for k in range(s.S):
            for y in range(s.YB):
                total = coef_bot[k * s.A * s.yb + y * s.q, d]
                for i in range(1, s.q):
                    total = total + coef_bot[k * s.A * s.yb + y * s.q + i, d]
                bot_faces[d, y, k * s.xb : (k + 1) * s.xb, :] = total

    got(gathered.at[pl.ds(0, others)], 10)
    chunk = s.A // s.NL
    for i in range(s.G):
        for k in range(s.NL):
            total = gathered[i * s.A + k * chunk]
            for j in range(1, chunk):
                total = total + gathered[i * s.A + k * chunk + j]
            bottom_all[i * s.xb : (i + 1) * s.xb, k * LANES : (k + 1) * LANES] = total
    everything = bottom_all[...]
    ready(7, 8, 9, 10, 11, 12, 13, 14)
    modes = right_parts(everything, to_modes[0], to_modes[1])
    modes = full_dot(qx_t[...], modes) * inverse[...]
    near = from_x[g]
    field = right_parts(full_dot(near[:, : s.NXB], modes), from_modes[0], from_modes[1])
    source = right_exact(full_dot(near[:, s.NXB :], everything), spread[...])
    planes = lambda wide: jnp.stack([wide[:, y * LANES : (y + 1) * LANES] for y in range(s.YB)])
    field = sweeps(planes(field), planes(source), [bot_faces[d] for d in range(3)], 0.25**s.merges)

    field = right_exact(field.reshape(s.YB * s.XBP, LANES), grow_z[...])
    field = left_exact(grow_x[...], field).reshape(s.YB, s.XMP, LANES)
    field = jnp.stack([field[y // 2] for y in range(s.YM)])
    got(res_side, 8)
    got(res_own.at[pl.ds(0, (s.A - 1) * s.ym)], 9)
    mid_res[...] = jnp.zeros(mid_res.shape, jnp.float32)
    mid_res[:, 0:SWEEPS, :] = res_side[0]
    mid_res[:, SWEEPS : SWEEPS + s.xm, :] = res_own[...]
    mid_res[:, SWEEPS + s.xm : 2 * SWEEPS + s.xm, :] = res_side[1]
    final[...] = sweeps(field, mid_res[...], [mid_faces[d] for d in range(3)], 0.25 ** (s.merges - 1))
    for y in range(s.ym):
        out[:, y, :] = final[a * s.ym + y, SWEEPS : SWEEPS + s.xm, : s.zm]

    sent = (
        x_high, x_high, x_high, y_low, y_high, coef_side, part, coef_bot.at[pl.ds(0, (s.S * s.A - 1) * s.yb)],
        res_side, res_own.at[pl.ds(0, (s.A - 1) * s.ym)], gathered.at[pl.ds(0, others)],
    )
    for kind, ref in enumerate(sent):
        got(ref, kind, send)


def local(s, constants, sol, src, fx, fy, fz):
    f32 = lambda *shape: pltpu.VMEM(shape, jnp.float32)
    total = s.G * s.A
    arrays = (sol, src, fx, fy, fz, *constants)
    result = pl.pallas_call(
        functools.partial(kernel, s, len(arrays)),
        out_shape=jax.ShapeDtypeStruct((s.xm, s.ym, s.zm), jnp.float32),
        in_specs=[pl.BlockSpec(memory_space=pltpu.HBM)] * len(arrays),
        out_specs=pl.BlockSpec(memory_space=pltpu.VMEM),
        scratch_shapes=[
            *[pltpu.VMEM(array.shape, array.dtype) for array in arrays],
            f32(2, s.Y, s.Z), f32(s.Y, s.Z), f32(2, s.X, s.Z), f32(s.X, s.Z), f32(2, s.X, s.Z), f32(s.X, s.Z),
            f32(s.YM, 3, s.xm, LANES), f32(2, s.YM, 3, SWEEPS, LANES), f32(2, s.ym, 3, SWEEPS, LANES),
            f32(s.S * s.A * s.yb, 3, s.xb, LANES),
            f32(s.YM, s.xm, LANES), f32(2, s.YM, SWEEPS, LANES), f32(2, s.ym, SWEEPS, LANES),
            f32(total, s.xb, LANES),
            f32(s.NXB, s.NL * LANES), f32(3, s.YM, s.XMP, LANES), f32(s.YM, s.XMP, LANES),
            f32(3, s.YB, s.XBP, LANES), f32(s.YM, s.XMP, LANES),
            pltpu.SemaphoreType.DMA((11,)),
            pltpu.SemaphoreType.DMA((11,)),
            pltpu.SemaphoreType.DMA((len(arrays),)),
        ],
        compiler_params=pltpu.CompilerParams(
            collective_id=0, has_side_effects=True
        ),
    )(*arrays)
    return result


def solution(mesh):
    groups, members = mesh.shape["grp"], mesh.shape["agg"]

    def whole(*arrays):
        nx, ny, nz = arrays[0].shape
        s = Sizes(groups, members, (nx // groups, ny // members, nz))
        constants = [jnp.asarray(t) for t in tables(s)]
        return jax.shard_map(
            functools.partial(local, s, constants),
            mesh=mesh,
            in_specs=(P("grp", "agg", None),) * 5,
            out_specs=P("grp", "agg", None),
            check_vma=False,
        )(*arrays)

    return whole
```
